32 devices in a mesh: groups: 2 (over y), outer: 2 (over x), inner: 4 (over z), head: 2 (over core).
Axes of the slice: x: 2, y: 2, z: 4, core: 2. Of those that a mesh axis runs over, the one named last changes fastest.
Arguments:
- queries: float32 [6144, 512], P(('groups', 'outer', 'inner'), 'head'), parts along dimension 0, may hold values from -5 to 5
- key_states: float32 [6144, 512], P(('groups', 'outer', 'inner'), 'head'), parts along dimension 0, may hold values from -5 to 5
- value_states: float32 [6144, 512], P(('groups', 'outer', 'inner'), 'head'), parts along dimension 0, may hold values from -5 to 5
- cotangent: bfloat16 [6144, 512], P(('groups', 'outer', 'inner'), 'head'), parts along dimension 0, may hold values from -5 to 5
Outputs:
- grad_queries: float32 [6144, 512], P(('groups', 'outer', 'inner'), 'head'), parts along dimension 0
- grad_keys: float32 [6144, 512], P(('groups', 'outer', 'inner'), 'head'), parts along dimension 0
- grad_values: float32 [6144, 512], P(('groups', 'outer', 'inner'), 'head'), parts along dimension 0
The draws below stay inside these ranges and needn't reach their ends.
There are 2 independent parts, one for each index of `groups`. The reference program is written for one: setup_inputs(seed, part) draws one part's arguments, and reference() takes and returns one part's arrays. A program takes and returns all parts, laid end to end along the dimension named above; each array names one. Nothing has to cross between parts.
All inputs are finite; a program needn't handle non-finite values.
Results may differ from the reference program's by a relative error of at most 0.0003.
Values sent between devices are 32-bit elements; how exact they have to be, the bound alone decides.
A program may use at most 64 MiB of HBM per device.

```python
import math
import jax
import jax.numpy as jnp
from jax import lax

HD = 128
HEADS = 4
SEG = 384
TOKENS = 3072


def segment_index():
    return jnp.arange(TOKENS) // SEG


def offsets(key, salt):
    table = jax.random.uniform(jax.random.fold_in(key, salt), (TOKENS // SEG, HEADS * HD), jnp.float32, -1.0, 1.0)
    return table[segment_index()]


def draw_queries(key, part):
    shape = (TOKENS, HEADS * HD)
    return jnp.clip(jax.random.normal(jax.random.fold_in(key, 11), shape, jnp.float32), -4.5, 4.5)


def draw_key_states(key, part):
    shape = (TOKENS, HEADS * HD)
    return jnp.clip(jax.random.normal(jax.random.fold_in(key, 12), shape, jnp.float32), -4.5, 4.5)


def draw_value_states(key, part):
    shape = (TOKENS, HEADS * HD)
    noise = jnp.clip(jax.random.normal(jax.random.fold_in(key, 13), shape, jnp.float32), -3.5, 3.5)
    return noise + offsets(key, 23)


def draw_cotangent(key, part):
    shape = (TOKENS, HEADS * HD)
    noise = jnp.clip(jax.random.normal(jax.random.fold_in(key, 14), shape, jnp.float32), -3.5, 3.5)
    return (noise + offsets(key, 24)).astype(jnp.bfloat16)


def setup_inputs(seed: int = 0, part: int = 0) -> dict:
    key_of = jax.random.split(jax.random.key(seed), 5)
    part_splits = jax.random.split(jax.random.fold_in(key_of[4], part), 5)
    return {
        "queries": draw_queries(jax.random.fold_in(jax.random.fold_in(key_of[4], part), 71), part),
        "key_states": draw_key_states(jax.random.fold_in(jax.random.fold_in(key_of[4], part), 71), part),
        "value_states": draw_value_states(jax.random.fold_in(jax.random.fold_in(key_of[4], part), 71), part),
        "cotangent": draw_cotangent(jax.random.fold_in(jax.random.fold_in(key_of[4], part), 71), part),
    }


def feature(inputs):
    return jax.nn.elu(inputs) + 1.0

def segment_step(carry, block):
    memory, znorm = carry
    query, keys, values = block
    highest = lax.Precision.HIGHEST
    feat_query = feature(query)
    feat_key = feature(keys)
    numer = jnp.einsum('thi,hij->thj', feat_query, memory, precision=highest)
    denom = jnp.maximum(jnp.einsum('thi,hi->th', feat_query, znorm, precision=highest), 1.0)
    reading = numer / denom[:, :, None]
    scores = jnp.einsum('thi,uhi->htu', query, keys, precision=highest) / math.sqrt(HD)
    causal = jnp.arange(SEG)[:, None] >= jnp.arange(SEG)[None, :]
    scores = jnp.where(causal[None], scores, -jnp.inf)
    probs = jax.nn.softmax(scores, axis=-1)
    local = jnp.einsum('htu,uhj->thj', probs, values, precision=highest)
    output = 0.5 * reading + 0.5 * local
    memory = memory + jnp.einsum('thi,thj->hij', feat_key, values, precision=highest)
    znorm = znorm + lax.optimization_barrier(jnp.sum(feat_key, axis=0))
    return ((memory, znorm), output)

def forward(queries, key_states, value_states):
    count = TOKENS // SEG
    shape = (count, SEG, HEADS, HD)
    start = (jnp.zeros((HEADS, HD, HD), jnp.float32), jnp.zeros((HEADS, HD), jnp.float32))
    final, outputs = lax.scan(segment_step, start, (queries.reshape(shape), key_states.reshape(shape), value_states.reshape(shape)))
    return outputs.reshape(TOKENS, HEADS * HD)

def reference(queries, key_states, value_states, cotangent):
    outputs, pullback = jax.vjp(forward, queries, key_states, value_states)
    grad_queries, grad_keys, grad_values = pullback(cotangent.astype(jnp.float32))
    return (grad_queries, grad_keys, grad_values)
```

```python
import functools
import math

import jax
import jax.numpy as jnp
from jax import lax
from jax.experimental import pallas as pl
from jax.experimental.pallas import tpu as pltpu
from jax.sharding import PartitionSpec as P

HD = 128
SEG = 384
BLK = 128
CHUNKS = 4
MESH = pl.DeviceIdType.MESH
F32 = jnp.float32


def dot(a, b, ca, cb):
    return lax.dot_general(
        a, b, (((ca,), (cb,)), ((), ())), precision=lax.Precision.HIGHEST, preferred_element_type=F32
    )


def feature(x):
    return jnp.where(x > 0, x + 1.0, jnp.exp(jnp.minimum(x, 0.0)))


class Chain:
    def __init__(self, reverse, n_o, n_i, refs):
        (self.own, self.acc, self.xin, self.y, self.fin, self.fout, self.bin, self.bout, self.sems) = refs
        o, i = lax.axis_index("outer"), lax.axis_index("inner")
        self.n_o, self.n_i = n_o, n_i
        self.o = n_o - 1 - o if reverse else o
        self.i = n_i - 1 - i if reverse else i
        self.b = n_i - 1 - self.i
        step = -1 if reverse else 1
        self.o_next = o + step
        self.i_next = i + step
        self.i_prev = i - step
        self.steps = CHUNKS + n_o - 1 + n_i - 1

    def copy(self, src, dst, kind, c, where):
        return pltpu.make_async_remote_copy(
            src_ref=src.at[c],
            dst_ref=dst.at[c],
            send_sem=self.sems.at[2 * kind, c],
            recv_sem=self.sems.at[2 * kind + 1, c],
            device_id=where,
            device_id_type=MESH,
        )

    def x_copy(self, c):
        return self.copy(self.y, self.xin, 0, c, {"outer": self.o_next})

    def f_copy(self, c):
        return self.copy(self.fout, self.fin, 1, c, {"inner": self.i_next})

    def b_copy(self, c):
        return self.copy(self.bout, self.bin, 2, c, {"inner": self.i_prev})

    def step(self, s):
        self.x_step(s - self.o)
        self.f_step(s - self.o - self.i)
        self.b_step(s - self.o - self.b)

    def x_step(self, c):
        @pl.when((c >= 0) & (c < CHUNKS))
        def _():
            @pl.when(self.o > 0)
            def _():
                self.x_copy(c).wait_recv()
                got = self.xin[c]
                self.acc[c] = got
                self.y[c] = got + self.own[c]

            @pl.when(self.o == 0)
            def _():
                self.acc[c] = jnp.zeros_like(self.acc[c])
                self.y[c] = self.own[c]

            @pl.when(self.o < self.n_o - 1)
            def _():
                self.x_copy(c).start()

    def f_step(self, c):
        @pl.when((c >= 0) & (c < CHUNKS))
        def _():
            @pl.when(self.i > 0)
            def _():
                self.f_copy(c).wait_recv()
                got = self.fin[c]
                self.acc[c] += got
                self.fout[c] = got + self.y[c]

            @pl.when(self.i == 0)
            def _():
                self.fout[c] = self.y[c]

            @pl.when(self.i < self.n_i - 1)
            def _():
                self.f_copy(c).start()

    def b_step(self, c):
        @pl.when((c >= 0) & (c < CHUNKS) & (self.o > 0))
        def _():
            @pl.when(self.b > 0)
            def _():
                self.b_copy(c).wait_recv()
                got = self.bin[c]
                self.acc[c] += got
                self.bout[c] = got + self.xin[c]

            @pl.when(self.b == 0)
            def _():
                self.bout[c] = self.xin[c]

            @pl.when(self.b < self.n_i - 1)
            def _():
                self.b_copy(c).start()

    def finish(self):
        def one(c, _):
            @pl.when(self.o < self.n_o - 1)
            def _():
                self.x_copy(c).wait_send()

            @pl.when(self.i < self.n_i - 1)
            def _():
                self.f_copy(c).wait_send()

            @pl.when((self.o > 0) & (self.b < self.n_i - 1))
            def _():
                self.b_copy(c).wait_send()

            return 0

        lax.fori_loop(0, CHUNKS, one, 0)


def kernel(n_o, n_i, heads, q_ref, k_ref, v_ref, ct_ref, gq_ref, gk_ref, gv_ref,
           fq_ref, fk_ref, dn_ref, zb, wb, zsem, wsem, *chain_refs):
    n = n_o * n_i
    o, i = lax.axis_index("outer"), lax.axis_index("inner")
    me = o * n_i + i
    barrier = pltpu.get_barrier_semaphore()

    def peer(d):
        p = lax.rem(me + d, n)
        return p, {"outer": p // n_i, "inner": lax.rem(p, n_i)}

    def greet(d, _):
        pl.semaphore_signal(barrier, inc=1, device_id=peer(d)[1], device_id_type=MESH)
        return 0

    lax.fori_loop(1, n, greet, 0)

    def spread_copy(buf, sem, slot, where):
        return pltpu.make_async_remote_copy(
            src_ref=buf.at[slot], dst_ref=buf.at[slot],
            send_sem=sem.at[0, slot], recv_sem=sem.at[1, slot],
            device_id=where, device_id_type=MESH,
        )

    def spread_start(buf, sem):
        def one(d, _):
            p, where = peer(d)
            pltpu.make_async_remote_copy(
                src_ref=buf.at[me], dst_ref=buf.at[me],
                send_sem=sem.at[0, p], recv_sem=sem.at[1, me],
                device_id=where, device_id_type=MESH,
            ).start()
            return 0

        lax.fori_loop(1, n, one, 0)

    def spread_wait(buf, sem):
        def one(d, _):
            p, where = peer(d)
            spread_copy(buf, sem, p, where).wait_recv()
            return 0

        lax.fori_loop(1, n, one, 0)

    def spread_finish(buf, sem):
        def one(d, _):
            p, where = peer(d)
            spread_copy(buf, sem, p, where).wait_send()
            return 0

        lax.fori_loop(1, n, one, 0)

    before = Chain(False, n_o, n_i, chain_refs[:9])
    after = Chain(True, n_o, n_i, chain_refs[9:])
    per = CHUNKS // heads
    rows = HD // per
    cols = [slice(h * HD, (h + 1) * HD) for h in range(heads)]

    def put(ref, h, value):
        for c in range(per):
            ref[h * per + c] = value[c * rows:(c + 1) * rows]

    def get(ref, h):
        return jnp.concatenate([ref[h * per + c] for c in range(per)], axis=0)

    sums = []
    for h in range(heads):
        fk = feature(k_ref[:, cols[h]])
        fk_ref[:, cols[h]] = fk
        sums.append(jnp.sum(fk, axis=0, keepdims=True))
    zb[me] = jnp.concatenate(sums, axis=0)
    pl.semaphore_wait(barrier, n - 1)
    spread_start(zb, zsem)
    for h in range(heads):
        put(before.own, h, dot(fk_ref[:, cols[h]], v_ref[:, cols[h]], 0, 0))
    before.step(0)

    for h in range(heads):
        fq_ref[:, cols[h]] = feature(q_ref[:, cols[h]])
    spread_wait(zb, zsem)
    slots = lax.broadcasted_iota(jnp.int32, (n, heads, HD), 0)
    znorm = jnp.sum(jnp.where(slots < me, zb[...], 0.0), axis=0)
    dens, raws = [], []
    for h in range(heads):
        fq = fq_ref[:, cols[h]]
        raw = jnp.sum(fq * znorm[h:h + 1], axis=1, keepdims=True)
        den = jnp.maximum(raw, 1.0)
        dn = (0.5 * ct_ref[:, cols[h]].astype(F32)) / den
        dn_ref[:, cols[h]] = dn
        raws.append(raw)
        dens.append(den)
        put(after.own, h, dot(fq, dn, 0, 0))

    scale = 1.0 / math.sqrt(HD)
    last = SEG // BLK - 1

    def attend(h, b):
        t, u = slice(b * BLK, (b + 1) * BLK), slice(0, (b + 1) * BLK)
        q, g = q_ref[t, cols[h]], 0.5 * ct_ref[t, cols[h]].astype(F32)
        k, v = k_ref[u, cols[h]], v_ref[u, cols[h]]
        s = dot(k, q, 1, 1) * scale
        size = (b + 1) * BLK
        row = lax.broadcasted_iota(jnp.int32, (size, BLK), 0)
        col = lax.broadcasted_iota(jnp.int32, (size, BLK), 1) + b * BLK
        s = jnp.where(row <= col, s, -jnp.inf)
        e = jnp.exp(s - jnp.max(s, axis=0, keepdims=True))
        p = e / jnp.sum(e, axis=0, keepdims=True)
        dp = dot(v, g, 1, 1)
        ds = p * (dp - jnp.sum(dp * p, axis=0, keepdims=True)) * scale
        gk, gv = dot(ds, q, 1, 0), dot(p, g, 1, 0)
        if b == last:
            gk_ref[u, cols[h]] = gk
            gv_ref[u, cols[h]] = gv
        else:
            gk_ref[u, cols[h]] += gk
            gv_ref[u, cols[h]] += gv
        gq_ref[t, cols[h]] = dot(ds, k, 0, 0)

    pieces = [(h, b) for h in range(heads) for b in range(last, -1, -1)]
    for s in range(1, before.steps + 1):
        if s < before.steps:
            before.step(s)
        after.step(s - 1)
        if pieces:
            attend(*pieces.pop(0))
    while pieces:
        attend(*pieces.pop(0))

    extra = []
    for h in range(heads):
        memory = get(before.acc, h)
        fq, dn = fq_ref[:, cols[h]], dn_ref[:, cols[h]]
        numer = dot(fq, memory, 1, 0)
        dden = jnp.where(raws[h] > 1.0, -jnp.sum(dn * numer, axis=1, keepdims=True) / dens[h], 0.0)
        extra.append(jnp.sum(fq * dden, axis=0, keepdims=True))
        grad = dot(dn, memory, 1, 1) + dden * znorm[h:h + 1]
        gq_ref[:, cols[h]] += grad * jnp.minimum(fq, 1.0)
    wb[me] = jnp.concatenate(extra, axis=0)
    spread_start(wb, wsem)
    later = []
    for h in range(heads):
        memory = get(after.acc, h)
        gv_ref[:, cols[h]] += dot(fk_ref[:, cols[h]], memory, 1, 0)
        later.append(dot(v_ref[:, cols[h]], memory, 1, 1))
    spread_wait(wb, wsem)
    lz = jnp.sum(jnp.where(slots > me, wb[...], 0.0), axis=0)
    for h in range(heads):
        gk_ref[:, cols[h]] += (later[h] + lz[h:h + 1]) * jnp.minimum(fk_ref[:, cols[h]], 1.0)
    before.finish()
    after.finish()
    spread_finish(zb, zsem)
    spread_finish(wb, wsem)


def shards(n_o, n_i, queries, key_states, value_states, cotangent):
    rows, columns = queries.shape
    assert rows == SEG
    heads = columns // HD
    n = n_o * n_i
    unit = pltpu.VMEM((CHUNKS, heads * HD // CHUNKS, HD), F32)
    chain = [unit] * 8 + [pltpu.SemaphoreType.DMA((6, CHUNKS))]
    full = pltpu.VMEM((rows, columns), F32)
    small = pltpu.VMEM((n, heads, HD), F32)
    vmem = pl.BlockSpec(memory_space=pltpu.VMEM)
    return tuple(pl.pallas_call(
        functools.partial(kernel, n_o, n_i, heads),
        out_shape=[jax.ShapeDtypeStruct((rows, columns), F32)] * 3,
        in_specs=[vmem] * 4,
        out_specs=[vmem] * 3,
        scratch_shapes=[full, full, full, small, small,
                        pltpu.SemaphoreType.DMA((2, n)), pltpu.SemaphoreType.DMA((2, n))] + chain + chain,
        compiler_params=pltpu.CompilerParams(
            collective_id=0, has_side_effects=True, vmem_limit_bytes=48 * 1024 * 1024
        ),
    )(queries, key_states, value_states, cotangent))


def solution(mesh):
    spec = P(("groups", "outer", "inner"), "head")
    body = functools.partial(shards, mesh.shape["outer"], mesh.shape["inner"])
    return jax.shard_map(body, mesh=mesh, in_specs=(spec,) * 4, out_specs=(spec,) * 3, check_vma=False)
```

```python
import functools
import math

import jax
import jax.numpy as jnp
from jax import lax
from jax.experimental import pallas as pl
from jax.experimental.pallas import tpu as pltpu
from jax.sharding import PartitionSpec as P

HD = 128
SEG = 384
BLK = 128
FILL = (1, 1, 1, 1)
MESH = pl.DeviceIdType.MESH
F32 = jnp.float32


def dot(a, b, ca, cb):
    return lax.dot_general(
        a, b, (((ca,), (cb,)), ((), ())), precision=lax.Precision.HIGHEST, preferred_element_type=F32
    )


def feature(x):
    return jnp.where(x > 0, x + 1.0, jnp.exp(jnp.minimum(x, 0.0)))


def kernel(n_o, n_i, heads, q_hbm, k_hbm, v_hbm, ct_hbm, gq_ref, gk_ref, gv_ref,
           q_ref, k_ref, v_ref, ct_ref, fq_ref, fk_ref, dn_ref, zb, wb,
           p_out, p_in, e_out, e_in, a_out, a_in, f_out, f_in, load_sem, sems):
    n = n_o * n_i
    me = lax.axis_index("outer") * n_i + lax.axis_index("inner")
    barrier = pltpu.get_barrier_semaphore()
    loads = [
        pltpu.make_async_copy(src, dst, load_sem.at[j])
        for j, (src, dst) in enumerate(((k_hbm, k_ref), (v_hbm, v_ref), (q_hbm, q_ref), (ct_hbm, ct_ref)))
    ]
    for load in loads:
        load.start()

    def peers(body):
        def one(d, _):
            p = lax.rem(me + d, n)
            body(p, {"outer": p // n_i, "inner": lax.rem(p, n_i)})
            return 0

        lax.fori_loop(1, n, one, 0)

    class Exchange:
        def __init__(self, kind, src, dst):
            self.kind, self.src, self.dst = kind, src, dst

        def copy(self, p, where, slot):
            return pltpu.make_async_remote_copy(
                src_ref=self.dst.at[me] if self.src is None else self.src.at[p],
                dst_ref=self.dst.at[slot],
                send_sem=sems.at[2 * self.kind, p],
                recv_sem=sems.at[2 * self.kind + 1, slot],
                device_id=where,
                device_id_type=MESH,
            )

        def start(self):
            peers(lambda p, where: self.copy(p, where, me).start())
            if self.src is not None:
                self.dst[me] = self.src[me]

        def wait(self):
            peers(lambda p, where: self.copy(p, where, p).wait_recv())

        def finish(self):
            peers(lambda p, where: self.copy(p, where, p).wait_send())

    z_ex, w_ex = Exchange(0, None, zb), Exchange(1, None, wb)
    p_ex, e_ex = Exchange(2, p_out, p_in), Exchange(3, e_out, e_in)
    a_ex, f_ex = Exchange(4, a_out, a_in), Exchange(5, f_out, f_in)

    peers(lambda p, where: pl.semaphore_signal(barrier, inc=1, device_id=where, device_id_type=MESH))

    per = n // heads
    rows = HD // per
    cols = [slice(h * HD, (h + 1) * HD) for h in range(heads)]

    def put(ref, h, value):
        for c in range(per):
            ref[h * per + c] = value[c * rows:(c + 1) * rows]

    def get(ref, h):
        return jnp.concatenate([ref[h * per + c] for c in range(per)], axis=0)

    sums = []
    loads[0].wait()
    for h in range(heads):
        fk = feature(k_ref[:, cols[h]])
        fk_ref[:, cols[h]] = fk
        sums.append(jnp.sum(fk, axis=0, keepdims=True))
    zb[me] = jnp.concatenate(sums, axis=0)
    loads[1].wait()
    for h in range(heads):
        put(p_out, h, dot(fk_ref[:, cols[h]], v_ref[:, cols[h]], 0, 0))
    loads[2].wait()
    for h in range(heads):
        fq_ref[:, cols[h]] = feature(q_ref[:, cols[h]])
    loads[3].wait()
    pl.semaphore_wait(barrier, n - 1)
    z_ex.start()
    p_ex.start()

    scale = 1.0 / math.sqrt(HD)
    last = SEG // BLK - 1

    def attend(h, b):
        t, u = slice(b * BLK, (b + 1) * BLK), slice(0, (b + 1) * BLK)
        q, g = q_ref[t, cols[h]], 0.5 * ct_ref[t, cols[h]].astype(F32)
        k, v = k_ref[u, cols[h]], v_ref[u, cols[h]]
        s = dot(k, q, 1, 1) * scale
        size = (b + 1) * BLK
        row = lax.broadcasted_iota(jnp.int32, (size, BLK), 0)
        col = lax.broadcasted_iota(jnp.int32, (size, BLK), 1) + b * BLK
        s = jnp.where(row <= col, s, -jnp.inf)
        e = jnp.exp(s - jnp.max(s, axis=0, keepdims=True))
        p = e / jnp.sum(e, axis=0, keepdims=True)
        dp = dot(v, g, 1, 1)
        ds = p * (dp - jnp.sum(dp * p, axis=0, keepdims=True)) * scale
        gk, gv = dot(ds, q, 1, 0), dot(p, g, 1, 0)
        if b == last:
            gk_ref[u, cols[h]] = gk
            gv_ref[u, cols[h]] = gv
        else:
            gk_ref[u, cols[h]] += gk
            gv_ref[u, cols[h]] += gv
        gq_ref[t, cols[h]] = dot(ds, k, 0, 0)

    pieces = [(h, b) for h in range(heads) for b in range(last, -1, -1)]

    def fill(count):
        for _ in range(count):
            attend(*pieces.pop(0))

    fill(FILL[0])
    z_ex.wait()
    slots = lax.broadcasted_iota(jnp.int32, (n, heads, HD), 0)
    znorm = jnp.sum(jnp.where(slots < me, zb[...], 0.0), axis=0)
    dens, raws = [], []
    for h in range(heads):
        fq = fq_ref[:, cols[h]]
        raw = jnp.sum(fq * znorm[h:h + 1], axis=1, keepdims=True)
        den = jnp.maximum(raw, 1.0)
        dn = (0.5 * ct_ref[:, cols[h]].astype(F32)) / den
        dn_ref[:, cols[h]] = dn
        raws.append(raw)
        dens.append(den)
        put(a_out, h, dot(fq, dn, 0, 0))
    a_ex.start()
    fill(FILL[1])
    p_ex.wait()
    total = jnp.zeros_like(p_in[0])
    for l in range(n):
        e_out[l] = total
        total = total + p_in[l]
    e_ex.start()
    fill(FILL[2])
    a_ex.wait()
    total = jnp.zeros_like(a_in[0])
    for l in range(n - 1, -1, -1):
        f_out[l] = total
        total = total + a_in[l]
    f_ex.start()
    fill(FILL[3])
    e_ex.wait()
    extra = []
    memories = []
    for h in range(heads):
        memory = get(e_in, h)
        memories.append(memory)
        fq = fq_ref[:, cols[h]]
        numer = dot(fq, memory, 1, 0)
        dden = jnp.where(raws[h] > 1.0, -jnp.sum(dn_ref[:, cols[h]] * numer, axis=1, keepdims=True) / dens[h], 0.0)
        dens[h] = dden
        extra.append(jnp.sum(fq * dden, axis=0, keepdims=True))
    wb[me] = jnp.concatenate(extra, axis=0)
    w_ex.start()
    fill(len(pieces))
    for h in range(heads):
        grad = dot(dn_ref[:, cols[h]], memories[h], 1, 1) + dens[h] * znorm[h:h + 1]
        gq_ref[:, cols[h]] += grad * jnp.minimum(fq_ref[:, cols[h]], 1.0)
    f_ex.wait()
    later = []
    for h in range(heads):
        memory = get(f_in, h)
        gv_ref[:, cols[h]] += dot(fk_ref[:, cols[h]], memory, 1, 0)
        later.append(dot(v_ref[:, cols[h]], memory, 1, 1))
    w_ex.wait()
    lz = jnp.sum(jnp.where(slots > me, wb[...], 0.0), axis=0)
    for h in range(heads):
        gk_ref[:, cols[h]] += (later[h] + lz[h:h + 1]) * jnp.minimum(fk_ref[:, cols[h]], 1.0)
    for ex in (z_ex, p_ex, a_ex, e_ex, f_ex, w_ex):
        ex.finish()


def shards(n_o, n_i, queries, key_states, value_states, cotangent):
    rows, columns = queries.shape
    assert rows == SEG
    heads = columns // HD
    n = n_o * n_i
    full = pltpu.VMEM((rows, columns), F32)
    small = pltpu.VMEM((n, heads, HD), F32)
    part = pltpu.VMEM((n, heads * HD // n, HD), F32)
    vmem = pl.BlockSpec(memory_space=pltpu.VMEM)
    hbm = pl.BlockSpec(memory_space=pltpu.HBM)
    return tuple(pl.pallas_call(
        functools.partial(kernel, n_o, n_i, heads),
        out_shape=[jax.ShapeDtypeStruct((rows, columns), F32)] * 3,
        in_specs=[hbm] * 4,
        out_specs=[vmem] * 3,
        scratch_shapes=[full, full, full, pltpu.VMEM((rows, columns), jnp.bfloat16), full, full, full,
                        small, small] + [part] * 8
        + [pltpu.SemaphoreType.DMA((4,)), pltpu.SemaphoreType.DMA((12, n))],
        compiler_params=pltpu.CompilerParams(
            collective_id=0, has_side_effects=True, vmem_limit_bytes=48 * 1024 * 1024
        ),
    )(queries, key_states, value_states, cotangent))


def solution(mesh):
    spec = P(("groups", "outer", "inner"), "head")
    body = functools.partial(shards, mesh.shape["outer"], mesh.shape["inner"])
    return jax.shard_map(body, mesh=mesh, in_specs=(spec,) * 4, out_specs=(spec,) * 3, check_vma=False)
```

```python
import functools
import math

import jax
import jax.numpy as jnp
from jax import lax
from jax.experimental import pallas as pl
from jax.experimental.pallas import tpu as pltpu
from jax.sharding import PartitionSpec as P

HD = 128
SEG = 384
BLK = 128
FILL = (1, 1, 1, 1)
MESH = pl.DeviceIdType.MESH
F32 = jnp.float32


def dot(a, b, ca, cb):
    return lax.dot_general(
        a, b, (((ca,), (cb,)), ((), ())), precision=lax.Precision.HIGHEST, preferred_element_type=F32
    )


def feature(x):
    return jnp.where(x > 0, x + 1.0, jnp.exp(jnp.minimum(x, 0.0)))


def kernel(n_o, n_i, heads, q_hbm, k_hbm, v_hbm, ct_hbm, gq_ref, gk_ref, gv_ref, fk_ref, v_ref, f_in, lz_ref,
           q_ref, k_ref, ct_ref, fq_ref, dn_ref, zb, wb,
           p_out, p_in, e_out, e_in, a_out, a_in, f_out, load_sem, sems):
    n = n_o * n_i
    me = lax.axis_index("outer") * n_i + lax.axis_index("inner")
    barrier = pltpu.get_barrier_semaphore()
    loads = [
        pltpu.make_async_copy(src, dst, load_sem.at[j])
        for j, (src, dst) in enumerate(((k_hbm, k_ref), (v_hbm, v_ref), (q_hbm, q_ref), (ct_hbm, ct_ref)))
    ]
    for load in loads:
        load.start()

    def peers(body):
        def one(d, _):
            p = lax.rem(me + d, n)
            body(p, {"outer": p // n_i, "inner": lax.rem(p, n_i)})
            return 0

        lax.fori_loop(1, n, one, 0, unroll=n <= 8)

    class Exchange:
        def __init__(self, kind, src, dst):
            self.kind, self.src, self.dst = kind, src, dst

        def copy(self, p, where, slot):
            return pltpu.make_async_remote_copy(
                src_ref=self.dst.at[me] if self.src is None else self.src.at[p],
                dst_ref=self.dst.at[slot],
                send_sem=sems.at[2 * self.kind, p],
                recv_sem=sems.at[2 * self.kind + 1, slot],
                device_id=where,
                device_id_type=MESH,
            )

        def start(self):
            peers(lambda p, where: self.copy(p, where, me).start())
            if self.src is not None:
                self.dst[me] = self.src[me]

        def wait(self):
            peers(lambda p, where: self.copy(p, where, p).wait_recv())

        def finish(self):
            peers(lambda p, where: self.copy(p, where, p).wait_send())

    z_ex, w_ex = Exchange(0, None, zb), Exchange(1, None, wb)
    p_ex, e_ex = Exchange(2, p_out, p_in), Exchange(3, e_out, e_in)
    a_ex, f_ex = Exchange(4, a_out, a_in), Exchange(5, f_out, f_in)

    peers(lambda p, where: pl.semaphore_signal(barrier, inc=1, device_id=where, device_id_type=MESH))

    per = n // heads
    rows = HD // per
    cols = [slice(h * HD, (h + 1) * HD) for h in range(heads)]

    def put(ref, h, value):
        for c in range(per):
            ref[h * per + c] = value[c * rows:(c + 1) * rows]

    def get(ref, h):
        return jnp.concatenate([ref[h * per + c] for c in range(per)], axis=0)

    sums = []
    loads[0].wait()
    for h in range(heads):
        fk = feature(k_ref[:, cols[h]])
        fk_ref[:, cols[h]] = fk
        sums.append(jnp.sum(fk, axis=0, keepdims=True))
    zb[me] = jnp.concatenate(sums, axis=0)
    loads[1].wait()
    for h in range(heads):
        put(p_out, h, dot(fk_ref[:, cols[h]], v_ref[:, cols[h]], 0, 0))
    loads[2].wait()
    for h in range(heads):
        fq_ref[:, cols[h]] = feature(q_ref[:, cols[h]])
    loads[3].wait()
    pl.semaphore_wait(barrier, n - 1)
    z_ex.start()
    p_ex.start()

    scale = 1.0 / math.sqrt(HD)
    last = SEG // BLK - 1

    def attend(h, b):
        t, u = slice(b * BLK, (b + 1) * BLK), slice(0, (b + 1) * BLK)
        q, g = q_ref[t, cols[h]], 0.5 * ct_ref[t, cols[h]].astype(F32)
        k, v = k_ref[u, cols[h]], v_ref[u, cols[h]]
        s = dot(k, q, 1, 1) * scale
        size = (b + 1) * BLK
        row = lax.broadcasted_iota(jnp.int32, (size, BLK), 0)
        col = lax.broadcasted_iota(jnp.int32, (size, BLK), 1) + b * BLK
        s = jnp.where(row <= col, s, -jnp.inf)
        e = jnp.exp(s - jnp.max(s, axis=0, keepdims=True))
        p = e / jnp.sum(e, axis=0, keepdims=True)
        dp = dot(v, g, 1, 1)
        ds = p * (dp - jnp.sum(dp * p, axis=0, keepdims=True)) * scale
        gk, gv = dot(ds, q, 1, 0), dot(p, g, 1, 0)
        if b == last:
            gk_ref[u, cols[h]] = gk
            gv_ref[u, cols[h]] = gv
        else:
            gk_ref[u, cols[h]] += gk
            gv_ref[u, cols[h]] += gv
        gq_ref[t, cols[h]] = dot(ds, k, 0, 0)

    pieces = [(h, b) for h in range(heads) for b in range(last, -1, -1)]

    def fill(count):
        for _ in range(count):
            attend(*pieces.pop(0))

    fill(FILL[0])
    z_ex.wait()
    slots = lax.broadcasted_iota(jnp.int32, (n, heads, HD), 0)
    znorm = jnp.sum(jnp.where(slots < me, zb[...], 0.0), axis=0)
    dens, raws = [], []
    for h in range(heads):
        fq = fq_ref[:, cols[h]]
        raw = jnp.sum(fq * znorm[h:h + 1], axis=1, keepdims=True)
        den = jnp.maximum(raw, 1.0)
        dn = (0.5 * ct_ref[:, cols[h]].astype(F32)) / den
        dn_ref[:, cols[h]] = dn
        raws.append(raw)
        dens.append(den)
        put(a_out, h, dot(fq, dn, 0, 0))
    a_ex.start()
    fill(FILL[1])
    p_ex.wait()
    total = jnp.zeros_like(p_in[0])
    for l in range(n):
        e_out[l] = total
        total = total + p_in[l]
    e_ex.start()
    fill(FILL[2])
    a_ex.wait()
    total = jnp.zeros_like(a_in[0])
    for l in range(n - 1, -1, -1):
        f_out[l] = total
        total = total + a_in[l]
    f_ex.start()
    fill(FILL[3])
    e_ex.wait()
    extra = []
    memories = []
    for h in range(heads):
        memory = get(e_in, h)
        memories.append(memory)
        fq = fq_ref[:, cols[h]]
        numer = dot(fq, memory, 1, 0)
        dden = jnp.where(raws[h] > 1.0, -jnp.sum(dn_ref[:, cols[h]] * numer, axis=1, keepdims=True) / dens[h], 0.0)
        dens[h] = dden
        extra.append(jnp.sum(fq * dden, axis=0, keepdims=True))
    wb[me] = jnp.concatenate(extra, axis=0)
    w_ex.start()
    fill(len(pieces))
    for h in range(heads):
        grad = dot(dn_ref[:, cols[h]], memories[h], 1, 1) + dens[h] * znorm[h:h + 1]
        gq_ref[:, cols[h]] += grad * jnp.minimum(fq_ref[:, cols[h]], 1.0)
    f_ex.wait()
    w_ex.wait()
    lz_ref[...] = jnp.sum(jnp.where(slots > me, wb[...], 0.0), axis=0)
    for ex in (z_ex, p_ex, a_ex, e_ex, f_ex, w_ex):
        ex.finish()


def closing(heads, gq_ref, gk_ref, gv_ref, fk_ref, v_ref, f_ref, lz_ref, gq_hbm, gk_hbm, gv_hbm, gk_out, gv_out, sems):
    stores = [
        pltpu.make_async_copy(src, dst, sems.at[j])
        for j, (src, dst) in enumerate(((gq_ref, gq_hbm), (gv_out, gv_hbm), (gk_out, gk_hbm)))
    ]
    stores[0].start()
    per = f_ref.shape[0] // heads
    cols = [slice(h * HD, (h + 1) * HD) for h in range(heads)]
    memories = [jnp.concatenate([f_ref[h * per + c] for c in range(per)], axis=0) for h in range(heads)]
    for h in range(heads):
        gv_out[:, cols[h]] = gv_ref[:, cols[h]] + dot(fk_ref[:, cols[h]], memories[h], 1, 0)
    stores[1].start()
    for h in range(heads):
        later = dot(v_ref[:, cols[h]], memories[h], 1, 1) + lz_ref[h:h + 1]
        gk_out[:, cols[h]] = gk_ref[:, cols[h]] + later * jnp.minimum(fk_ref[:, cols[h]], 1.0)
    stores[2].start()
    for store in stores:
        store.wait()


def shards(n_o, n_i, queries, key_states, value_states, cotangent):
    rows, columns = queries.shape
    assert rows == SEG
    heads = columns // HD
    n = n_o * n_i
    full = pltpu.VMEM((rows, columns), F32)
    small = pltpu.VMEM((n, heads, HD), F32)
    part = pltpu.VMEM((n, heads * HD // n, HD), F32)
    vmem = pl.BlockSpec(memory_space=pltpu.VMEM)
    hbm = pl.BlockSpec(memory_space=pltpu.HBM)
    array = jax.ShapeDtypeStruct((rows, columns), F32)
    held = [array] * 5 + [jax.ShapeDtypeStruct(part.shape, F32), jax.ShapeDtypeStruct((heads, HD), F32)]
    parts = pl.pallas_call(
        functools.partial(kernel, n_o, n_i, heads),
        out_shape=held,
        in_specs=[hbm] * 4,
        out_specs=[vmem] * 7,
        scratch_shapes=[full, full, pltpu.VMEM((rows, columns), jnp.bfloat16), full, full,
                        small, small] + [part] * 7
        + [pltpu.SemaphoreType.DMA((4,)), pltpu.SemaphoreType.DMA((12, n))],
        compiler_params=pltpu.CompilerParams(
            collective_id=0, has_side_effects=True, vmem_limit_bytes=48 * 1024 * 1024
        ),
    )(*(pltpu.with_memory_space_constraint(x, pltpu.HBM) for x in (queries, key_states, value_states, cotangent)))
    return tuple(pl.pallas_call(
        functools.partial(closing, heads),
        out_shape=[array] * 3,
        in_specs=[vmem] * 7,
        out_specs=[hbm] * 3,
        scratch_shapes=[full, full, pltpu.SemaphoreType.DMA((3,))],
        compiler_params=pltpu.CompilerParams(vmem_limit_bytes=24 * 1024 * 1024),
    )(*parts))


def solution(mesh):
    spec = P(("groups", "outer", "inner"), "head")
    body = functools.partial(shards, mesh.shape["outer"], mesh.shape["inner"])
    return jax.shard_map(body, mesh=mesh, in_specs=(spec,) * 4, out_specs=(spec,) * 3, check_vma=False)
```

```python
import functools
import math

import jax
import jax.numpy as jnp
from jax import lax
from jax.experimental import pallas as pl
from jax.experimental.pallas import tpu as pltpu
from jax.sharding import PartitionSpec as P

HD = 128
SEG = 384
BLK = 128
FILL = (1, 2, 1, 1)
MESH = pl.DeviceIdType.MESH
F32 = jnp.float32


def dot(a, b, ca, cb):
    return lax.dot_general(
        a, b, (((ca,), (cb,)), ((), ())), precision=lax.Precision.HIGHEST, preferred_element_type=F32
    )


def feature(x):
    return jnp.where(x > 0, x + 1.0, jnp.exp(jnp.minimum(x, 0.0)))


def kernel(n_o, n_i, heads, q_hbm, k_hbm, v_hbm, ct_hbm, gq_ref, gk_ref, gv_ref, fk_ref, v_ref, f_in, lz_ref,
           q_ref, k_ref, ct_ref, fq_ref, dn_ref, zb, wb,
           p_out, p_in, e_out, e_in, a_out, a_in, f_out, load_sem, sems):
    n = n_o * n_i
    me = lax.axis_index("outer") * n_i + lax.axis_index("inner")
    barrier = pltpu.get_barrier_semaphore()
    loads = [
        pltpu.make_async_copy(src, dst, load_sem.at[j])
        for j, (src, dst) in enumerate(((k_hbm, k_ref), (v_hbm, v_ref), (q_hbm, q_ref), (ct_hbm, ct_ref)))
    ]
    for load in loads:
        load.start()

    def peers(body):
        def one(d, _):
            p = lax.rem(me + d, n)
            body(p, {"outer": p // n_i, "inner": lax.rem(p, n_i)})
            return 0

        lax.fori_loop(1, n, one, 0, unroll=n <= 8)

    class Exchange:
        def __init__(self, kind, src, dst, idle_from=-1, idle_to=-1):
            self.kind, self.src, self.dst = kind, src, dst
            self.idle_from, self.idle_to = idle_from, idle_to

        def used(self, sender, receiver, act):
            if self.idle_from >= 0:
                pl.when(sender != self.idle_from)(act)
            elif self.idle_to >= 0:
                pl.when(receiver != self.idle_to)(act)
            else:
                act()

        def copy(self, p, where, slot):
            return pltpu.make_async_remote_copy(
                src_ref=self.dst.at[me] if self.src is None else self.src.at[p],
                dst_ref=self.dst.at[slot],
                send_sem=sems.at[2 * self.kind, p],
                recv_sem=sems.at[2 * self.kind + 1, slot],
                device_id=where,
                device_id_type=MESH,
            )

        def start(self):
            peers(lambda p, where: self.used(me, p, lambda: self.copy(p, where, me).start()))
            if self.idle_to >= 0:
                @pl.when(me == self.idle_to)
                def _():
                    self.dst[...] = jnp.zeros_like(self.dst)

            if self.src is not None:
                self.dst[me] = self.src[me]

        def wait(self):
            peers(lambda p, where: self.used(p, me, lambda: self.copy(p, where, p).wait_recv()))

        def finish(self):
            peers(lambda p, where: self.used(me, p, lambda: self.copy(p, where, p).wait_send()))

    z_ex, w_ex = Exchange(0, None, zb), Exchange(1, None, wb)
    p_ex, e_ex = Exchange(2, p_out, p_in, idle_from=n - 1), Exchange(3, e_out, e_in, idle_to=0)
    a_ex, f_ex = Exchange(4, a_out, a_in, idle_from=0), Exchange(5, f_out, f_in, idle_to=n - 1)

    peers(lambda p, where: pl.semaphore_signal(barrier, inc=1, device_id=where, device_id_type=MESH))

    per = n // heads
    rows = HD // per
    cols = [slice(h * HD, (h + 1) * HD) for h in range(heads)]

    def put(ref, h, value):
        for c in range(per):
            ref[h * per + c] = value[c * rows:(c + 1) * rows]

    def get(ref, h):
        return jnp.concatenate([ref[h * per + c] for c in range(per)], axis=0)

    sums = []
    loads[0].wait()
    for h in range(heads):
        fk = feature(k_ref[:, cols[h]])
        fk_ref[:, cols[h]] = fk
        sums.append(jnp.sum(fk, axis=0, keepdims=True))
    zb[me] = jnp.concatenate(sums, axis=0)
    loads[1].wait()
    for h in range(heads):
        put(p_out, h, dot(fk_ref[:, cols[h]], v_ref[:, cols[h]], 0, 0))
    loads[2].wait()
    for h in range(heads):
        fq_ref[:, cols[h]] = feature(q_ref[:, cols[h]])
    loads[3].wait()
    pl.semaphore_wait(barrier, n - 1)
    z_ex.start()
    p_ex.start()

    scale = 1.0 / math.sqrt(HD)
    last = SEG // BLK - 1

    def attend(h, b):
        t, u = slice(b * BLK, (b + 1) * BLK), slice(0, (b + 1) * BLK)
        q, g = q_ref[t, cols[h]], 0.5 * ct_ref[t, cols[h]].astype(F32)
        k, v = k_ref[u, cols[h]], v_ref[u, cols[h]]
        s = dot(k, q, 1, 1) * scale
        size = (b + 1) * BLK
        row = lax.broadcasted_iota(jnp.int32, (size, BLK), 0)
        col = lax.broadcasted_iota(jnp.int32, (size, BLK), 1) + b * BLK
        s = jnp.where(row <= col, s, -jnp.inf)
        e = jnp.exp(s - jnp.max(s, axis=0, keepdims=True))
        p = e / jnp.sum(e, axis=0, keepdims=True)
        dp = dot(v, g, 1, 1)
        ds = p * (dp - jnp.sum(dp * p, axis=0, keepdims=True)) * scale
        gk, gv = dot(ds, q, 1, 0), dot(p, g, 1, 0)
        if b == last:
            gk_ref[u, cols[h]] = gk
            gv_ref[u, cols[h]] = gv
        else:
            gk_ref[u, cols[h]] += gk
            gv_ref[u, cols[h]] += gv
        gq_ref[t, cols[h]] = dot(ds, k, 0, 0)

    pieces = [(h, b) for h in range(heads) for b in range(last, -1, -1)]

    def fill(count):
        for _ in range(count):
            attend(*pieces.pop(0))

    fill(FILL[0])
    z_ex.wait()
    slots = lax.broadcasted_iota(jnp.int32, (n, heads, HD), 0)
    znorm = jnp.sum(jnp.where(slots < me, zb[...], 0.0), axis=0)
    dens, raws = [], []
    for h in range(heads):
        fq = fq_ref[:, cols[h]]
        raw = jnp.sum(fq * znorm[h:h + 1], axis=1, keepdims=True)
        den = jnp.maximum(raw, 1.0)
        dn = (0.5 * ct_ref[:, cols[h]].astype(F32)) / den
        dn_ref[:, cols[h]] = dn
        raws.append(raw)
        dens.append(den)
        put(a_out, h, dot(fq, dn, 0, 0))
    a_ex.start()
    fill(FILL[1])
    p_ex.wait()
    total = jnp.zeros_like(p_in[0])
    for l in range(n):
        e_out[l] = total
        if l < n - 1:
            total = total + p_in[l]
    e_ex.start()
    fill(FILL[2])
    a_ex.wait()
    total = jnp.zeros_like(a_in[0])
    for l in range(n - 1, -1, -1):
        f_out[l] = total
        if l > 0:
            total = total + a_in[l]
    f_ex.start()
    fill(FILL[3])
    e_ex.wait()
    extra = []
    memories = []
    for h in range(heads):
        memory = get(e_in, h)
        memories.append(memory)
        fq = fq_ref[:, cols[h]]
        numer = dot(fq, memory, 1, 0)
        dden = jnp.where(raws[h] > 1.0, -jnp.sum(dn_ref[:, cols[h]] * numer, axis=1, keepdims=True) / dens[h], 0.0)
        dens[h] = dden
        extra.append(jnp.sum(fq * dden, axis=0, keepdims=True))
    wb[me] = jnp.concatenate(extra, axis=0)
    w_ex.start()
    fill(len(pieces))
    for h in range(heads):
        grad = dot(dn_ref[:, cols[h]], memories[h], 1, 1) + dens[h] * znorm[h:h + 1]
        gq_ref[:, cols[h]] += grad * jnp.minimum(fq_ref[:, cols[h]], 1.0)
    f_ex.wait()
    w_ex.wait()
    lz_ref[...] = jnp.sum(jnp.where(slots > me, wb[...], 0.0), axis=0)
    for ex in (z_ex, p_ex, a_ex, e_ex, f_ex, w_ex):
        ex.finish()


def closing(heads, gq_ref, gk_ref, gv_ref, fk_ref, v_ref, f_ref, lz_ref, gq_hbm, gk_hbm, gv_hbm, gk_out, gv_out, sems):
    stores = [
        pltpu.make_async_copy(src, dst, sems.at[j])
        for j, (src, dst) in enumerate(((gq_ref, gq_hbm), (gv_out, gv_hbm), (gk_out, gk_hbm)))
    ]
    stores[0].start()
    per = f_ref.shape[0] // heads
    cols = [slice(h * HD, (h + 1) * HD) for h in range(heads)]
    memories = [jnp.concatenate([f_ref[h * per + c] for c in range(per)], axis=0) for h in range(heads)]
    for h in range(heads):
        gv_out[:, cols[h]] = gv_ref[:, cols[h]] + dot(fk_ref[:, cols[h]], memories[h], 1, 0)
    stores[1].start()
    for h in range(heads):
        later = dot(v_ref[:, cols[h]], memories[h], 1, 1) + lz_ref[h:h + 1]
        gk_out[:, cols[h]] = gk_ref[:, cols[h]] + later * jnp.minimum(fk_ref[:, cols[h]], 1.0)
    stores[2].start()
    for store in stores:
        store.wait()


def shards(n_o, n_i, queries, key_states, value_states, cotangent):
    rows, columns = queries.shape
    assert rows == SEG
    heads = columns // HD
    n = n_o * n_i
    full = pltpu.VMEM((rows, columns), F32)
    small = pltpu.VMEM((n, heads, HD), F32)
    part = pltpu.VMEM((n, heads * HD // n, HD), F32)
    vmem = pl.BlockSpec(memory_space=pltpu.VMEM)
    hbm = pl.BlockSpec(memory_space=pltpu.HBM)
    array = jax.ShapeDtypeStruct((rows, columns), F32)
    held = [array] * 5 + [jax.ShapeDtypeStruct(part.shape, F32), jax.ShapeDtypeStruct((heads, HD), F32)]
    parts = pl.pallas_call(
        functools.partial(kernel, n_o, n_i, heads),
        out_shape=held,
        in_specs=[hbm] * 4,
        out_specs=[vmem] * 7,
        scratch_shapes=[full, full, pltpu.VMEM((rows, columns), jnp.bfloat16), full, full,
                        small, small] + [part] * 7
        + [pltpu.SemaphoreType.DMA((4,)), pltpu.SemaphoreType.DMA((12, n))],
        compiler_params=pltpu.CompilerParams(
            collective_id=0, has_side_effects=True, vmem_limit_bytes=48 * 1024 * 1024
        ),
    )(*(pltpu.with_memory_space_constraint(x, pltpu.HBM) for x in (queries, key_states, value_states, cotangent)))
    return tuple(pl.pallas_call(
        functools.partial(closing, heads),
        out_shape=[array] * 3,
        in_specs=[vmem] * 7,
        out_specs=[hbm] * 3,
        scratch_shapes=[full, full, pltpu.SemaphoreType.DMA((3,))],
        compiler_params=pltpu.CompilerParams(vmem_limit_bytes=24 * 1024 * 1024),
    )(*parts))


def solution(mesh):
    spec = P(("groups", "outer", "inner"), "head")
    body = functools.partial(shards, mesh.shape["outer"], mesh.shape["inner"])
    return jax.shard_map(body, mesh=mesh, in_specs=(spec,) * 4, out_specs=(spec,) * 3, check_vma=False)
```
